32 devices in a mesh: fsdp: 8 (over y, x, core), sp: 4 (over z).
Axes of the slice: x: 2, y: 2, z: 4, core: 2. Of those that a mesh axis runs over, the one named last changes fastest.
Arguments:
- inputs: bfloat16 [8, 1024, 768], P('fsdp', 'sp'), may hold values from -6 to 6
- w_qkv: bfloat16 [2, 768, 3, 768], P(None, 'fsdp'), may hold values from -0.21875 to 0.21875
- w_out: bfloat16 [2, 768, 768], P(None, 'fsdp'), may hold values from -0.875 to 0.875
- w_up: bfloat16 [2, 768, 3072], P(None, 'fsdp'), may hold values from -0.21875 to 0.21875
- w_down: bfloat16 [2, 3072, 768], P(None, 'fsdp'), may hold values from -0.109375 to 0.109375
- norm_gain: bfloat16 [2, 2, 768], P(None, None, 'fsdp'), may hold values from 0.5 to 1.5
- norm_shift: bfloat16 [2, 2, 768], P(None, None, 'fsdp'), may hold values from -4 to 4
- qv_bias: bfloat16 [2, 2, 768], P(None, None, 'fsdp'), may hold values from -4 to 4
- branch_bias: bfloat16 [2, 2, 768], P(None, None, 'fsdp'), may hold values from -4 to 4
- up_bias: bfloat16 [2, 3072], P(None, 'fsdp'), may hold values from -6 to 6
- cotangent: bfloat16 [8, 1024, 768], P('fsdp', 'sp'), may hold values from -6 to 6
Outputs:
- output: bfloat16 [8, 1024, 768], P('fsdp', 'sp')
- grad_inputs: bfloat16 [8, 1024, 768], P('fsdp', 'sp')
- grad_w_qkv: float32 [2, 768, 3, 768], P(None, 'fsdp')
- grad_w_out: float32 [2, 768, 768], P(None, 'fsdp')
- grad_w_up: float32 [2, 768, 3072], P(None, 'fsdp')
- grad_w_down: float32 [2, 3072, 768], P(None, 'fsdp')
- grad_norm_gain: float32 [2, 2, 768], P(None, None, 'fsdp')
- grad_norm_shift: float32 [2, 2, 768], P(None, None, 'fsdp')
- grad_qv_bias: float32 [2, 2, 768], P(None, None, 'fsdp')
- grad_branch_bias: float32 [2, 2, 768], P(None, None, 'fsdp')
- grad_up_bias: float32 [2, 3072], P(None, 'fsdp')
The draws below stay inside these ranges and needn't reach their ends.
All inputs are finite; a program needn't handle non-finite values.
Results may differ from the reference program's by a relative error of at most 0.014.
Values may be sent and summed in bfloat16 or wider, within the bound.
A program may use at most 256 MiB of HBM per device.

```python
import jax
import jax.numpy as jnp
from jax import lax

D = 768
HEADS = 12
HD = 64
FF = 3072
LAYERS = 2
FRAMES = 1024
ALL_CLIPS = 8


def levels(rng, dims, cuts, low, largest):
    level = 1.0
    for dim, parts in cuts:
        steps = jax.random.uniform(jax.random.fold_in(jax.random.fold_in(rng, 6), dim), (parts,), jnp.float32, low / len(cuts), largest / len(cuts))
        level = level * jnp.repeat(jnp.exp(steps), dims[dim] // parts).reshape((-1,) + (1,) * (len(dims) - 1 - dim))
    return level


def gaussian(own_key, shape, scale, reach, cuts=(), dtype=jnp.bfloat16):
    drawn = jax.random.normal(own_key, shape, jnp.float32) * scale
    if len(cuts) > 0:
        drawn = levels(own_key, shape, cuts, -0.22, 0.18) * drawn
    return jnp.clip(drawn, min=-reach, max=reach).astype(dtype)


def setup_inputs(seed: int = 0) -> dict:
    key_of = jax.random.split(jax.random.key(seed), 12)
    return {
        "inputs": gaussian(key_of[0], (ALL_CLIPS, FRAMES, D), 1.0, 6.0, ((0, 8), (1, 4))),
        "w_qkv": gaussian(key_of[1], (LAYERS, D, 3, D), D ** -0.5, 0.21875, ((1, 8),)),
        "w_out": gaussian(key_of[2], (LAYERS, D, D), (D // 16) ** -0.5, 0.875, ((1, 8),)),
        "w_up": gaussian(key_of[3], (LAYERS, D, FF), D ** -0.5, 0.21875, ((1, 8),)),
        "w_down": gaussian(key_of[4], (LAYERS, FF, D), FF ** -0.5, 0.109375, ((1, 8),)),
        "norm_gain": jnp.clip(1.0 + 0.1 * jax.random.normal(key_of[5], (LAYERS, 2, D), jnp.float32), 0.5, 1.5).astype(jnp.bfloat16),
        "norm_shift": gaussian(key_of[6], (LAYERS, 2, D), 0.3, 4.0, ((2, 8),)),
        "qv_bias": gaussian(key_of[7], (LAYERS, 2, D), 0.3, 4.0, ((2, 8),)),
        "branch_bias": gaussian(key_of[8], (LAYERS, 2, D), 0.3, 4.0, ((2, 8),)),
        "up_bias": gaussian(key_of[9], (LAYERS, FF), 0.5, 6.0, ((1, 8),)),
        "cotangent": gaussian(key_of[10], (ALL_CLIPS, FRAMES, D), 1.0, 6.0, ((0, 8), (1, 4))),
    }


HIGH = lax.Precision.HIGHEST
epsilon = 1e-05

@jax.custom_vjp
def low(v):
    return lax.optimization_barrier(v.astype(jnp.bfloat16)).astype(jnp.float32)

@jax.custom_vjp
def low_back(v):
    return v

def low_keep(v):
    return (low(v), None)

def low_pass(kept, grad):
    return (grad,)

def back_keep(v):
    return (v, None)

def back_low(kept, grad):
    return (low(grad),)
low.defvjp(low_keep, low_pass)
low_back.defvjp(back_keep, back_low)

def norm_rows(values, gain, shift):
    center = values - lax.optimization_barrier(jnp.mean(values, axis=-1, keepdims=True))
    variance = lax.optimization_barrier(jnp.mean(center * center, axis=-1, keepdims=True))
    return center * lax.rsqrt(variance + epsilon) * gain + shift

def matmul_high(left, right):
    return jnp.dot(left, right, precision=HIGH)

def encoder_layer(stream, weights_one):
    weight_qkv, weight_out, weight_up, weight_down, gains, shifts, attn_bias, branch, up_shift = weights_one
    normed = low(norm_rows(stream, gains[0], shifts[0]))
    bias_qkv = jnp.concatenate([attn_bias[0], jnp.zeros_like(attn_bias[0]), attn_bias[1]])
    projected = low_back(low(matmul_high(normed, weight_qkv.reshape(D, 3 * D)) + bias_qkv))
    projected = projected.reshape(FRAMES, 3, HEADS, HD)
    queries = projected[:, 0]
    key_rows = projected[:, 1]
    value_rows = projected[:, 2]
    scores = low_back(jnp.einsum('qhd,khd->hqk', queries, key_rows, precision=HIGH) * HD ** (-0.5))
    attention = low(jax.nn.softmax(scores, axis=-1))
    mixed_rows = jnp.einsum('hqk,khd->qhd', attention, value_rows, precision=HIGH).reshape(FRAMES, D)
    mixed_rows = low_back(low(mixed_rows))
    middle = stream + low_back(matmul_high(mixed_rows, weight_out) + branch[0])
    normed_two = low(norm_rows(middle, gains[1], shifts[1]))
    pre_act = low_back(matmul_high(normed_two, weight_up) + up_shift)
    activated = low(jax.nn.gelu(pre_act, approximate=False))
    return middle + low_back(matmul_high(activated, weight_down) + branch[1])

def reference(inputs, w_qkv, w_out, w_up, w_down, norm_gain, norm_shift, qv_bias, branch_bias, up_bias, cotangent):
    weights_all = tuple((array.astype(jnp.float32) for array in (w_qkv, w_out, w_up, w_down, norm_gain, norm_shift, qv_bias, branch_bias, up_bias)))

    def forward(weights_now, stream):
        for layer_index in range(LAYERS):
            stream = encoder_layer(stream, tuple((array[layer_index] for array in weights_now)))
        return stream

    def per_clip(totals, clip_pair):
        clip_in, clip_grad = clip_pair
        result, pull = jax.vjp(forward, weights_all, clip_in.astype(jnp.float32))
        grad_weights, grad_clip = pull(clip_grad.astype(jnp.float32))
        totals = jax.tree.map(jnp.add, totals, grad_weights)
        return (totals, (result.astype(jnp.bfloat16), grad_clip.astype(jnp.bfloat16)))
    start_totals = jax.tree.map(jnp.zeros_like, weights_all)
    totals, (results, grad_clips) = lax.scan(per_clip, start_totals, (inputs, cotangent))
    return (results, grad_clips, totals[0], totals[1], totals[2], totals[3], totals[4], totals[5], totals[6], totals[7], totals[8])
```

```python
import jax
import jax.numpy as jnp
from jax import lax
from jax.sharding import PartitionSpec as P

HD = 64
LAYERS = 2


epsilon = 1e-05


def norm_rows(values, gain, shift):
    center = values - jnp.mean(values, axis=-1, keepdims=True)
    variance = jnp.mean(center * center, axis=-1, keepdims=True)
    return center * lax.rsqrt(variance + epsilon) * gain + shift


def gelu_exact(values):
    return jax.nn.gelu(values, approximate=False)


def product(left, right):
    return jnp.dot(left, right, preferred_element_type=jnp.float32)


def product_back(left, right):
    return jnp.einsum("te,fe->tf", left, right, preferred_element_type=jnp.float32)


def outer_sum(left, right):
    return jnp.einsum("td,te->de", left, right, preferred_element_type=jnp.float32)


def column_sums(values):
    return jnp.sum(values.astype(jnp.float32), axis=0)


def gather_rows(shard):
    return lax.all_gather(shard, "fsdp", axis=0, tiled=True)


def log_two(size):
    return size.bit_length() - 1


def exchange_halves(parts, axis_name, bit, axis):
    size = lax.axis_size(axis_name)
    mine = (lax.axis_index(axis_name) >> bit) & 1
    kept = lax.dynamic_index_in_dim(parts, mine, axis, keepdims=False)
    sent = lax.dynamic_index_in_dim(parts, 1 - mine, axis, keepdims=False)
    got = lax.ppermute(sent, axis_name, [(i, i ^ (1 << bit)) for i in range(size)])
    return (kept.astype(jnp.float32) + got.astype(jnp.float32)).astype(jnp.bfloat16)


def reduce_owner(grads, order):
    size = lax.axis_size("fsdp")
    bits = log_two(size)
    parts = grads.reshape((2,) * bits + (grads.shape[0] // size, grads.shape[1]))
    left = list(range(bits - 1, -1, -1))
    for bit in order:
        axis = left.index(bit)
        left.pop(axis)
        parts = exchange_halves(parts, "fsdp", bit, axis)
    return parts


def reduce_frames(grads, axis):
    size = lax.axis_size("sp")
    bits = log_two(size)
    shape = grads.shape
    parts = grads.reshape(
        shape[:axis] + (2,) * bits + (shape[axis] // size,) + shape[axis + 1 :]
    )
    for bit in range(bits):
        parts = exchange_halves(parts, "sp", bit, axis + bits - 1 - bit)
    return lax.all_gather(parts, "sp", axis=axis, tiled=True)


def settle(grads, axis):
    bits = log_two(lax.axis_size("fsdp"))
    half = grads.shape[1] // 2
    forward = [0] + list(range(1, bits))
    backward = [0] + list(range(bits - 1, 0, -1))
    low = grads.astype(jnp.bfloat16)
    first = reduce_owner(low[:, :half], forward)
    second = reduce_owner(low[:, half:], backward)
    return reduce_frames(jnp.concatenate([first, second], axis=1), axis)


def attend(query_rows, key_rows, value_rows):
    clips, length, local_heads, head_size = query_rows.shape
    block = min(512, length)
    scale = head_size ** (-0.5)

    def one_block(start):
        query_block = lax.dynamic_slice_in_dim(query_rows, start, block, 1)
        scores = (
            jnp.einsum("cqhd,ckhd->chqk", query_block, key_rows, preferred_element_type=jnp.float32)
            * scale
        )
        highest = jnp.max(scores, axis=-1, keepdims=True)
        powered = jnp.exp(scores - highest)
        summed = jnp.sum(powered, axis=-1, keepdims=True)
        weights_low = (powered / summed).astype(jnp.bfloat16)
        mixed = jnp.einsum(
            "chqk,ckhd->cqhd", weights_low, value_rows, preferred_element_type=jnp.float32
        )
        return (mixed.astype(jnp.bfloat16), (highest + jnp.log(summed))[..., 0])

    starts = jnp.arange(length // block, dtype=jnp.int32) * block
    mixed, log_total = lax.map(one_block, starts)
    mixed = jnp.moveaxis(mixed, 0, 1).reshape(clips, length, local_heads, head_size)
    log_total = jnp.moveaxis(log_total, 0, 2).reshape(clips, local_heads, length)
    return (mixed, log_total)


def attend_back(query_rows, key_rows, value_rows, log_total, grad_mixed):
    clips, length, local_heads, head_size = query_rows.shape
    block = min(512, length)
    scale = head_size ** (-0.5)

    def one_block(carry, start):
        grad_keys, grad_values = carry
        query_block = lax.dynamic_slice_in_dim(query_rows, start, block, 1)
        grad_block = lax.dynamic_slice_in_dim(grad_mixed, start, block, 1)
        total_block = lax.dynamic_slice_in_dim(log_total, start, block, 2)
        scores = (
            jnp.einsum("cqhd,ckhd->chqk", query_block, key_rows, preferred_element_type=jnp.float32)
            * scale
        )
        weights_full = jnp.exp(scores - total_block[..., None])
        grad_weights = jnp.einsum(
            "cqhd,ckhd->chqk", grad_block, value_rows, preferred_element_type=jnp.float32
        )
        inner = jnp.sum(weights_full * grad_weights, axis=-1, keepdims=True)
        grad_scores = (weights_full * (grad_weights - inner)).astype(jnp.bfloat16)
        grad_query = (
            jnp.einsum("chqk,ckhd->cqhd", grad_scores, key_rows, preferred_element_type=jnp.float32)
            * scale
        )
        grad_keys = (
            grad_keys
            + jnp.einsum(
                "chqk,cqhd->ckhd", grad_scores, query_block, preferred_element_type=jnp.float32
            )
            * scale
        )
        grad_values = grad_values + jnp.einsum(
            "chqk,cqhd->ckhd",
            weights_full.astype(jnp.bfloat16),
            grad_block,
            preferred_element_type=jnp.float32,
        )
        return ((grad_keys, grad_values), grad_query.astype(jnp.bfloat16))

    starts = jnp.arange(length // block, dtype=jnp.int32) * block
    zeros_start = jnp.zeros(key_rows.shape, jnp.float32)
    (grad_keys, grad_values), grad_query = lax.scan(one_block, (zeros_start, zeros_start), starts)
    grad_query = jnp.moveaxis(grad_query, 0, 1).reshape(clips, length, local_heads, head_size)
    return (grad_query, grad_keys.astype(jnp.bfloat16), grad_values.astype(jnp.bfloat16))


def local(
    inputs,
    w_qkv,
    w_out,
    w_up,
    w_down,
    norm_gain,
    norm_shift,
    qv_bias,
    branch_bias,
    up_bias,
    cotangent,
):
    clips, frames, width = inputs.shape
    groups = lax.axis_size("sp")
    length = frames * groups
    hidden = w_up.shape[2]
    local_heads = width // groups // HD
    rows_all = clips * frames
    stream = inputs.astype(jnp.float32).reshape(rows_all, width)
    kept = []
    shard = w_out.shape[1]
    vectors = jnp.concatenate(
        [
            part
            for l in range(LAYERS)
            for part in (
                norm_gain[l].T,
                norm_shift[l].T,
                qv_bias[l].T,
                branch_bias[l].T,
                up_bias[l].reshape(shard, -1),
            )
        ],
        axis=1,
    )
    count = vectors.shape[1] // LAYERS
    spare = 128 - vectors.shape[1]
    first = jnp.concatenate(
        [w_qkv[0].reshape(shard, -1), jnp.pad(vectors, ((0, 0), (0, spare)))], axis=1
    )
    first = gather_rows(first)
    vectors = first[:, 3 * width :]
    for layer_index in range(LAYERS):
        if layer_index == 0:
            weight_qkv = first[:, : 3 * width]
        else:
            weight_qkv = gather_rows(w_qkv[layer_index].reshape(shard, -1))
        weight_out = gather_rows(w_out[layer_index])
        weight_up = gather_rows(w_up[layer_index])
        weight_down = gather_rows(w_down[layer_index])
        vector_full = vectors[:, layer_index * count : (layer_index + 1) * count].astype(
            jnp.float32
        )
        gains = vector_full[:, 0:2]
        shifts = vector_full[:, 2:4]
        attn_bias = vector_full[:, 4:6]
        branch = vector_full[:, 6:8]
        up_shift = vector_full[:, 8:].reshape(hidden)
        normed = norm_rows(stream, gains[:, 0], shifts[:, 0]).astype(jnp.bfloat16)
        bias_qkv = jnp.concatenate(
            [attn_bias[:, 0], jnp.zeros((width,), jnp.float32), attn_bias[:, 1]]
        )
        projected = (product(normed, weight_qkv) + bias_qkv).astype(jnp.bfloat16)
        heads = lax.all_to_all(
            projected.reshape(clips, frames, 3, groups, width // groups),
            "sp",
            split_axis=3,
            concat_axis=1,
            tiled=True,
        )
        heads = heads.reshape(clips, length, 3, local_heads, HD)
        query_rows = heads[:, :, 0]
        key_rows = heads[:, :, 1]
        value_rows = heads[:, :, 2]
        mixed, log_total = attend(query_rows, key_rows, value_rows)
        returned = lax.all_to_all(
            mixed.reshape(clips, length, 1, width // groups),
            "sp",
            split_axis=1,
            concat_axis=2,
            tiled=True,
        )
        mixed_rows = returned.reshape(rows_all, width)
        middle = stream + product(mixed_rows, weight_out) + branch[:, 0]
        normed_two = norm_rows(middle, gains[:, 1], shifts[:, 1]).astype(jnp.bfloat16)
        pre_act = product(normed_two, weight_up) + up_shift
        activated = gelu_exact(pre_act).astype(jnp.bfloat16)
        kept.append(
            (
                stream,
                weight_qkv,
                weight_out,
                weight_up,
                weight_down,
                gains,
                shifts,
                normed,
                query_rows,
                key_rows,
                value_rows,
                log_total,
                mixed_rows,
                middle,
                normed_two,
                pre_act,
                activated,
            )
        )
        stream = middle + product(activated, weight_down) + branch[:, 1]
    output = stream.astype(jnp.bfloat16).reshape(clips, frames, width)
    grad_stream = cotangent.astype(jnp.float32).reshape(rows_all, width)
    layer_grads = []
    vector_sums = []
    for layer_index in reversed(range(LAYERS)):
        (
            layer_input,
            weight_qkv,
            weight_out,
            weight_up,
            weight_down,
            gains,
            shifts,
            normed,
            query_rows,
            key_rows,
            value_rows,
            log_total,
            mixed_rows,
            middle,
            normed_two,
            pre_act,
            activated,
        ) = kept[layer_index]
        grad_branch = grad_stream.astype(jnp.bfloat16)
        grad_down = settle(outer_sum(activated, grad_branch), 0)
        grad_down_bias = column_sums(grad_branch)
        grad_act = product_back(grad_branch, weight_down)
        grad_pre = jax.vjp(gelu_exact, pre_act)[1](grad_act)[0].astype(jnp.bfloat16)
        grad_up = settle(outer_sum(normed_two, grad_pre), 1)
        grad_up_bias = column_sums(grad_pre)
        grad_norm_two = product_back(grad_pre, weight_up)
        norm_pull = jax.vjp(norm_rows, middle, gains[:, 1], shifts[:, 1])[1]
        grad_middle, grad_gain_two, grad_shift_two = norm_pull(grad_norm_two)
        grad_middle = grad_middle + grad_stream
        grad_branch_one = grad_middle.astype(jnp.bfloat16)
        grad_out = outer_sum(mixed_rows, grad_branch_one)
        grad_out_bias = column_sums(grad_branch_one)
        grad_mixed = product_back(grad_branch_one, weight_out).astype(jnp.bfloat16)
        grad_heads = lax.all_to_all(
            grad_mixed.reshape(clips, frames, groups, width // groups),
            "sp",
            split_axis=2,
            concat_axis=1,
            tiled=True,
        )
        grad_heads = grad_heads.reshape(clips, length, local_heads, HD)
        grad_query, grad_key, grad_value = attend_back(
            query_rows, key_rows, value_rows, log_total, grad_heads
        )
        stacked = jnp.stack([grad_query, grad_key, grad_value], axis=2).reshape(
            clips, length, 3, 1, width // groups
        )
        grad_proj = lax.all_to_all(stacked, "sp", split_axis=1, concat_axis=3, tiled=True).reshape(
            rows_all, 3 * width
        )
        grad_qkv = outer_sum(normed, grad_proj)
        proj_sums = column_sums(grad_proj)
        grad_norm_one = product_back(grad_proj, weight_qkv)
        norm_pull = jax.vjp(norm_rows, layer_input, gains[:, 0], shifts[:, 0])[1]
        grad_input, grad_gain_one, grad_shift_one = norm_pull(grad_norm_one)
        grad_stream = grad_middle + grad_input
        grad_attn = settle(jnp.concatenate([grad_qkv, grad_out], axis=1), 1)
        vector_grads = jnp.concatenate(
            [
                jnp.stack([grad_gain_one, grad_gain_two], axis=1),
                jnp.stack([grad_shift_one, grad_shift_two], axis=1),
                jnp.stack([proj_sums[:width], proj_sums[2 * width :]], axis=1),
                jnp.stack([grad_out_bias, grad_down_bias], axis=1),
                grad_up_bias.reshape(width, hidden // width),
            ],
            axis=1,
        )
        layer_grads.append((grad_attn, grad_up, grad_down))
        vector_sums.append(vector_grads)
    layer_grads = layer_grads[::-1]
    grad_inputs = grad_stream.astype(jnp.bfloat16).reshape(clips, frames, width)
    qkv_list, out_list, up_list, down_list = ([], [], [], [])
    gain_list, shift_list, bias_list, branch_list, upbias_list = ([], [], [], [], [])
    vector_sums = lax.psum(jnp.concatenate(vector_sums[::-1], axis=1), ("fsdp", "sp"))
    vector_sums = lax.dynamic_slice_in_dim(
        vector_sums, lax.axis_index("fsdp") * shard, shard, 0
    )
    for layer_index, (attn_part, up_part, down_part) in enumerate(layer_grads):
        vector_part = vector_sums[:, layer_index * count : (layer_index + 1) * count]
        attn_part = attn_part.astype(jnp.float32)
        qkv_list.append(attn_part[:, : 3 * width].reshape(shard, 3, width))
        out_list.append(attn_part[:, 3 * width :])
        up_list.append(up_part.astype(jnp.float32))
        down_list.append(down_part.astype(jnp.float32))
        gain_list.append(vector_part[:, 0:2].T)
        shift_list.append(vector_part[:, 2:4].T)
        bias_list.append(vector_part[:, 4:6].T)
        branch_list.append(vector_part[:, 6:8].T)
        upbias_list.append(vector_part[:, 8:].reshape(-1))
    return (
        output,
        grad_inputs,
        jnp.stack(qkv_list),
        jnp.stack(out_list),
        jnp.stack(up_list),
        jnp.stack(down_list),
        jnp.stack(gain_list),
        jnp.stack(shift_list),
        jnp.stack(bias_list),
        jnp.stack(branch_list),
        jnp.stack(upbias_list),
    )


def solution(mesh):
    placed = (
        P("fsdp", "sp", None),
        P(None, "fsdp", None, None),
        P(None, "fsdp", None),
        P(None, "fsdp", None),
        P(None, "fsdp", None),
        P(None, None, "fsdp"),
        P(None, None, "fsdp"),
        P(None, None, "fsdp"),
        P(None, None, "fsdp"),
        P(None, "fsdp"),
        P("fsdp", "sp", None),
    )
    return jax.shard_map(
        local,
        mesh=mesh,
        in_specs=placed,
        out_specs=(
            P("fsdp", "sp", None),
            P("fsdp", "sp", None),
            P(None, "fsdp", None, None),
            P(None, "fsdp", None),
            P(None, "fsdp", None),
            P(None, "fsdp", None),
            P(None, None, "fsdp"),
            P(None, None, "fsdp"),
            P(None, None, "fsdp"),
            P(None, None, "fsdp"),
            P(None, "fsdp"),
        ),
        check_vma=False,
    )
```

```python
import jax
import jax.numpy as jnp
from jax import lax
from jax.sharding import PartitionSpec as P

HD = 64
LAYERS = 2


epsilon = 1e-05


def norm_rows(values, gain, shift):
    center = values - jnp.mean(values, axis=-1, keepdims=True)
    variance = jnp.mean(center * center, axis=-1, keepdims=True)
    return center * lax.rsqrt(variance + epsilon) * gain + shift


def gelu_exact(values):
    return jax.nn.gelu(values, approximate=False)


def product(left, right):
    return jnp.dot(left, right, preferred_element_type=jnp.float32)


def product_back(left, right):
    return jnp.einsum("te,fe->tf", left, right, preferred_element_type=jnp.float32)


def outer_sum(left, right):
    return jnp.einsum("td,te->de", left, right, preferred_element_type=jnp.float32)


def column_sums(values):
    return jnp.sum(values.astype(jnp.float32), axis=0)


def gather_rows(shard):
    return lax.all_gather(shard, "fsdp", axis=0, tiled=True)


def log_two(size):
    return size.bit_length() - 1


def exchange_halves(parts, axis_name, bit, axis):
    size = lax.axis_size(axis_name)
    mine = (lax.axis_index(axis_name) >> bit) & 1
    kept = lax.dynamic_index_in_dim(parts, mine, axis, keepdims=False)
    sent = lax.dynamic_index_in_dim(parts, 1 - mine, axis, keepdims=False)
    got = lax.ppermute(sent, axis_name, [(i, i ^ (1 << bit)) for i in range(size)])
    return (kept.astype(jnp.float32) + got.astype(jnp.float32)).astype(parts.dtype)


def gather_halves(part, axis_name, bit, axis):
    size = lax.axis_size(axis_name)
    mine = (lax.axis_index(axis_name) >> bit) & 1
    got = lax.ppermute(part, axis_name, [(i, i ^ (1 << bit)) for i in range(size)])
    return jnp.stack(
        [jnp.where(mine == 0, part, got), jnp.where(mine == 0, got, part)], axis=axis
    )


def reduce_owner(grads, order):
    size = lax.axis_size("fsdp")
    bits = log_two(size)
    parts = grads.reshape((2,) * bits + (grads.shape[0] // size, grads.shape[1]))
    left = list(range(bits - 1, -1, -1))
    for bit in order:
        axis = left.index(bit)
        left.pop(axis)
        parts = exchange_halves(parts, "fsdp", bit, axis)
    return parts


def reduce_frames(grads, axis):
    size = lax.axis_size("sp")
    bits = log_two(size)
    shape = grads.shape
    parts = grads.reshape(
        shape[:axis] + (2,) * bits + (shape[axis] // size,) + shape[axis + 1 :]
    )
    for bit in range(bits):
        parts = exchange_halves(parts, "sp", bit, axis + bits - 1 - bit)
    for bit in reversed(range(bits)):
        parts = gather_halves(parts, "sp", bit, axis + bits - 1 - bit)
    return parts.reshape(shape)


def settle_vectors(grads):
    size = lax.axis_size("fsdp")
    bits = log_two(size)
    parts = grads.reshape((2,) * bits + grads.shape[1:])
    for bit in range(bits):
        parts = exchange_halves(parts, "fsdp", bit, bits - 1 - bit)
    groups = lax.axis_size("sp")
    for bit in range(log_two(groups)):
        parts = parts + lax.ppermute(parts, "sp", [(i, i ^ (1 << bit)) for i in range(groups)])
    return parts


def settle(grads, axis):
    bits = log_two(lax.axis_size("fsdp"))
    half = grads.shape[1] // 2
    forward = [0] + list(range(1, bits))
    backward = [0] + list(range(bits - 1, 0, -1))
    low = grads.astype(jnp.bfloat16)
    first = reduce_owner(low[:, :half], forward)
    second = reduce_owner(low[:, half:], backward)
    return reduce_frames(jnp.concatenate([first, second], axis=1), axis)


def attend(query_rows, key_rows, value_rows):
    clips, length, local_heads, head_size = query_rows.shape
    block = min(512, length)
    scale = head_size ** (-0.5)

    def one_block(start):
        query_block = lax.dynamic_slice_in_dim(query_rows, start, block, 1)
        scores = (
            jnp.einsum("cqhd,ckhd->chqk", query_block, key_rows, preferred_element_type=jnp.float32)
            * scale
        )
        highest = jnp.max(scores, axis=-1, keepdims=True)
        powered = jnp.exp(scores - highest)
        summed = jnp.sum(powered, axis=-1, keepdims=True)
        weights_low = (powered / summed).astype(jnp.bfloat16)
        mixed = jnp.einsum(
            "chqk,ckhd->cqhd", weights_low, value_rows, preferred_element_type=jnp.float32
        )
        return (mixed.astype(jnp.bfloat16), (highest + jnp.log(summed))[..., 0])

    starts = jnp.arange(length // block, dtype=jnp.int32) * block
    mixed, log_total = lax.map(one_block, starts)
    mixed = jnp.moveaxis(mixed, 0, 1).reshape(clips, length, local_heads, head_size)
    log_total = jnp.moveaxis(log_total, 0, 2).reshape(clips, local_heads, length)
    return (mixed, log_total)


def attend_back(query_rows, key_rows, value_rows, log_total, grad_mixed):
    clips, length, local_heads, head_size = query_rows.shape
    block = min(512, length)
    scale = head_size ** (-0.5)

    def one_block(carry, start):
        grad_keys, grad_values = carry
        query_block = lax.dynamic_slice_in_dim(query_rows, start, block, 1)
        grad_block = lax.dynamic_slice_in_dim(grad_mixed, start, block, 1)
        total_block = lax.dynamic_slice_in_dim(log_total, start, block, 2)
        scores = (
            jnp.einsum("cqhd,ckhd->chqk", query_block, key_rows, preferred_element_type=jnp.float32)
            * scale
        )
        weights_full = jnp.exp(scores - total_block[..., None])
        grad_weights = jnp.einsum(
            "cqhd,ckhd->chqk", grad_block, value_rows, preferred_element_type=jnp.float32
        )
        inner = jnp.sum(weights_full * grad_weights, axis=-1, keepdims=True)
        grad_scores = (weights_full * (grad_weights - inner)).astype(jnp.bfloat16)
        grad_query = (
            jnp.einsum("chqk,ckhd->cqhd", grad_scores, key_rows, preferred_element_type=jnp.float32)
            * scale
        )
        grad_keys = (
            grad_keys
            + jnp.einsum(
                "chqk,cqhd->ckhd", grad_scores, query_block, preferred_element_type=jnp.float32
            )
            * scale
        )
        grad_values = grad_values + jnp.einsum(
            "chqk,cqhd->ckhd",
            weights_full.astype(jnp.bfloat16),
            grad_block,
            preferred_element_type=jnp.float32,
        )
        return ((grad_keys, grad_values), grad_query.astype(jnp.bfloat16))

    starts = jnp.arange(length // block, dtype=jnp.int32) * block
    zeros_start = jnp.zeros(key_rows.shape, jnp.float32)
    (grad_keys, grad_values), grad_query = lax.scan(one_block, (zeros_start, zeros_start), starts)
    grad_query = jnp.moveaxis(grad_query, 0, 1).reshape(clips, length, local_heads, head_size)
    return (grad_query, grad_keys.astype(jnp.bfloat16), grad_values.astype(jnp.bfloat16))


def local(
    inputs,
    w_qkv,
    w_out,
    w_up,
    w_down,
    norm_gain,
    norm_shift,
    qv_bias,
    branch_bias,
    up_bias,
    cotangent,
):
    clips, frames, width = inputs.shape
    groups = lax.axis_size("sp")
    length = frames * groups
    hidden = w_up.shape[2]
    local_heads = width // groups // HD
    rows_all = clips * frames
    stream = inputs.astype(jnp.float32).reshape(rows_all, width)
    kept = []
    shard = w_out.shape[1]
    vectors = jnp.concatenate(
        [
            part
            for l in range(LAYERS)
            for part in (
                norm_gain[l].T,
                norm_shift[l].T,
                qv_bias[l].T,
                branch_bias[l].T,
                up_bias[l].reshape(shard, -1),
            )
        ],
        axis=1,
    )
    count = vectors.shape[1] // LAYERS
    spare = 128 - vectors.shape[1]
    first = jnp.concatenate(
        [w_qkv[0].reshape(shard, -1), jnp.pad(vectors, ((0, 0), (0, spare)))], axis=1
    )
    first = gather_rows(first)
    vectors = first[:, 3 * width :]
    for layer_index in range(LAYERS):
        if layer_index == 0:
            weight_qkv = first[:, : 3 * width]
        else:
            weight_qkv = gather_rows(w_qkv[layer_index].reshape(shard, -1))
        weight_out = gather_rows(w_out[layer_index])
        weight_up = gather_rows(w_up[layer_index])
        weight_down = gather_rows(w_down[layer_index])
        vector_full = vectors[:, layer_index * count : (layer_index + 1) * count].astype(
            jnp.float32
        )
        gains = vector_full[:, 0:2]
        shifts = vector_full[:, 2:4]
        attn_bias = vector_full[:, 4:6]
        branch = vector_full[:, 6:8]
        up_shift = vector_full[:, 8:].reshape(hidden)
        normed = norm_rows(stream, gains[:, 0], shifts[:, 0]).astype(jnp.bfloat16)
        bias_qkv = jnp.concatenate(
            [attn_bias[:, 0], jnp.zeros((width,), jnp.float32), attn_bias[:, 1]]
        )
        projected = (product(normed, weight_qkv) + bias_qkv).astype(jnp.bfloat16)
        heads = lax.all_to_all(
            projected.reshape(clips, frames, 3, groups, width // groups),
            "sp",
            split_axis=3,
            concat_axis=1,
            tiled=True,
        )
        heads = heads.reshape(clips, length, 3, local_heads, HD)
        query_rows = heads[:, :, 0]
        key_rows = heads[:, :, 1]
        value_rows = heads[:, :, 2]
        mixed, log_total = attend(query_rows, key_rows, value_rows)
        returned = lax.all_to_all(
            mixed.reshape(clips, length, 1, width // groups),
            "sp",
            split_axis=1,
            concat_axis=2,
            tiled=True,
        )
        mixed_rows = returned.reshape(rows_all, width)
        middle = stream + product(mixed_rows, weight_out) + branch[:, 0]
        normed_two = norm_rows(middle, gains[:, 1], shifts[:, 1]).astype(jnp.bfloat16)
        pre_act = product(normed_two, weight_up) + up_shift
        activated = gelu_exact(pre_act).astype(jnp.bfloat16)
        kept.append(
            (
                stream,
                weight_qkv,
                weight_out,
                weight_up,
                weight_down,
                gains,
                shifts,
                normed,
                query_rows,
                key_rows,
                value_rows,
                log_total,
                mixed_rows,
                middle,
                normed_two,
                pre_act,
                activated,
            )
        )
        stream = middle + product(activated, weight_down) + branch[:, 1]
    output = stream.astype(jnp.bfloat16).reshape(clips, frames, width)
    grad_stream = cotangent.astype(jnp.float32).reshape(rows_all, width)
    layer_grads = []
    vector_sums = []
    for layer_index in reversed(range(LAYERS)):
        (
            layer_input,
            weight_qkv,
            weight_out,
            weight_up,
            weight_down,
            gains,
            shifts,
            normed,
            query_rows,
            key_rows,
            value_rows,
            log_total,
            mixed_rows,
            middle,
            normed_two,
            pre_act,
            activated,
        ) = kept[layer_index]
        grad_branch = grad_stream.astype(jnp.bfloat16)
        grad_down = settle(outer_sum(activated, grad_branch), 0)
        grad_down_bias = column_sums(grad_branch)
        grad_act = product_back(grad_branch, weight_down)
        grad_pre = jax.vjp(gelu_exact, pre_act)[1](grad_act)[0].astype(jnp.bfloat16)
        grad_up = settle(outer_sum(normed_two, grad_pre), 1)
        grad_up_bias = column_sums(grad_pre)
        grad_norm_two = product_back(grad_pre, weight_up)
        norm_pull = jax.vjp(norm_rows, middle, gains[:, 1], shifts[:, 1])[1]
        grad_middle, grad_gain_two, grad_shift_two = norm_pull(grad_norm_two)
        grad_middle = grad_middle + grad_stream
        grad_branch_one = grad_middle.astype(jnp.bfloat16)
        grad_out = outer_sum(mixed_rows, grad_branch_one)
        grad_out_bias = column_sums(grad_branch_one)
        grad_mixed = product_back(grad_branch_one, weight_out).astype(jnp.bfloat16)
        grad_heads = lax.all_to_all(
            grad_mixed.reshape(clips, frames, groups, width // groups),
            "sp",
            split_axis=2,
            concat_axis=1,
            tiled=True,
        )
        grad_heads = grad_heads.reshape(clips, length, local_heads, HD)
        grad_query, grad_key, grad_value = attend_back(
            query_rows, key_rows, value_rows, log_total, grad_heads
        )
        stacked = jnp.stack([grad_query, grad_key, grad_value], axis=2).reshape(
            clips, length, 3, 1, width // groups
        )
        grad_proj = lax.all_to_all(stacked, "sp", split_axis=1, concat_axis=3, tiled=True).reshape(
            rows_all, 3 * width
        )
        grad_qkv = outer_sum(normed, grad_proj)
        proj_sums = column_sums(grad_proj)
        grad_norm_one = product_back(grad_proj, weight_qkv)
        norm_pull = jax.vjp(norm_rows, layer_input, gains[:, 0], shifts[:, 0])[1]
        grad_input, grad_gain_one, grad_shift_one = norm_pull(grad_norm_one)
        grad_stream = grad_middle + grad_input
        grad_attn = settle(jnp.concatenate([grad_qkv, grad_out], axis=1), 1)
        vector_grads = jnp.concatenate(
            [
                grad_gain_one,
                grad_gain_two,
                grad_shift_one,
                grad_shift_two,
                proj_sums[:width],
                proj_sums[2 * width :],
                grad_out_bias,
                grad_down_bias,
            ]
        ).reshape(8, -1, shard)
        vector_grads = jnp.concatenate(
            [jnp.swapaxes(vector_grads, 0, 1), grad_up_bias.reshape(width // shard, -1, shard)],
            axis=1,
        )
        layer_grads.append((grad_attn, grad_up, grad_down))
        vector_sums.append(vector_grads)
    layer_grads = layer_grads[::-1]
    grad_inputs = grad_stream.astype(jnp.bfloat16).reshape(clips, frames, width)
    qkv_list, out_list, up_list, down_list = ([], [], [], [])
    gain_list, shift_list, bias_list, branch_list, upbias_list = ([], [], [], [], [])
    vector_sums = settle_vectors(jnp.concatenate(vector_sums[::-1], axis=1))
    for layer_index, (attn_part, up_part, down_part) in enumerate(layer_grads):
        vector_part = vector_sums[layer_index * count : (layer_index + 1) * count]
        attn_part = attn_part.astype(jnp.float32)
        qkv_list.append(attn_part[:, : 3 * width].reshape(shard, 3, width))
        out_list.append(attn_part[:, 3 * width :])
        up_list.append(up_part.astype(jnp.float32))
        down_list.append(down_part.astype(jnp.float32))
        gain_list.append(vector_part[0:2])
        shift_list.append(vector_part[2:4])
        bias_list.append(vector_part[4:6])
        branch_list.append(vector_part[6:8])
        upbias_list.append(vector_part[8:].reshape(-1))
    return (
        output,
        grad_inputs,
        jnp.stack(qkv_list),
        jnp.stack(out_list),
        jnp.stack(up_list),
        jnp.stack(down_list),
        jnp.stack(gain_list),
        jnp.stack(shift_list),
        jnp.stack(bias_list),
        jnp.stack(branch_list),
        jnp.stack(upbias_list),
    )


def solution(mesh):
    placed = (
        P("fsdp", "sp", None),
        P(None, "fsdp", None, None),
        P(None, "fsdp", None),
        P(None, "fsdp", None),
        P(None, "fsdp", None),
        P(None, None, "fsdp"),
        P(None, None, "fsdp"),
        P(None, None, "fsdp"),
        P(None, None, "fsdp"),
        P(None, "fsdp"),
        P("fsdp", "sp", None),
    )
    return jax.shard_map(
        local,
        mesh=mesh,
        in_specs=placed,
        out_specs=(
            P("fsdp", "sp", None),
            P("fsdp", "sp", None),
            P(None, "fsdp", None, None),
            P(None, "fsdp", None),
            P(None, "fsdp", None),
            P(None, "fsdp", None),
            P(None, None, "fsdp"),
            P(None, None, "fsdp"),
            P(None, None, "fsdp"),
            P(None, None, "fsdp"),
            P(None, "fsdp"),
        ),
        check_vma=False,
    )
```

```python
import jax
import jax.numpy as jnp
from jax import lax
from jax.experimental import pallas as pl
from jax.experimental.pallas import tpu as pltpu
from jax.sharding import PartitionSpec as P

HD = 64
LAYERS = 2


epsilon = 1e-05


def norm_rows(values, gain, shift):
    center = values - jnp.mean(values, axis=-1, keepdims=True)
    variance = jnp.mean(center * center, axis=-1, keepdims=True)
    return center * lax.rsqrt(variance + epsilon) * gain + shift


def gelu_exact(values):
    return jax.nn.gelu(values, approximate=False)


def product(left, right):
    return jnp.dot(left, right, preferred_element_type=jnp.float32)


def product_back(left, right):
    return jnp.einsum("te,fe->tf", left, right, preferred_element_type=jnp.float32)


def outer_sum(left, right):
    return jnp.einsum("td,te->de", left, right, preferred_element_type=jnp.float32)


def column_sums(values):
    return jnp.sum(values.astype(jnp.float32), axis=0)


def gather_rows(shard):
    return lax.all_gather(shard, "fsdp", axis=0, tiled=True)


def log_two(size):
    return size.bit_length() - 1


def exchange_halves(parts, axis_name, bit, axis):
    size = lax.axis_size(axis_name)
    mine = (lax.axis_index(axis_name) >> bit) & 1
    kept = lax.dynamic_index_in_dim(parts, mine, axis, keepdims=False)
    sent = lax.dynamic_index_in_dim(parts, 1 - mine, axis, keepdims=False)
    got = lax.ppermute(sent, axis_name, [(i, i ^ (1 << bit)) for i in range(size)])
    return (kept.astype(jnp.float32) + got.astype(jnp.float32)).astype(parts.dtype)


def gather_halves(part, axis_name, bit, axis):
    size = lax.axis_size(axis_name)
    mine = (lax.axis_index(axis_name) >> bit) & 1
    got = lax.ppermute(part, axis_name, [(i, i ^ (1 << bit)) for i in range(size)])
    return jnp.stack(
        [jnp.where(mine == 0, part, got), jnp.where(mine == 0, got, part)], axis=axis
    )


def reduce_owner(grads, order):
    size = lax.axis_size("fsdp")
    bits = log_two(size)
    parts = grads.reshape((2,) * bits + (grads.shape[0] // size, grads.shape[1]))
    left = list(range(bits - 1, -1, -1))
    for bit in order:
        axis = left.index(bit)
        left.pop(axis)
        parts = exchange_halves(parts, "fsdp", bit, axis)
    return parts


def reduce_frames(grads, axis):
    size = lax.axis_size("sp")
    bits = log_two(size)
    shape = grads.shape
    parts = grads.reshape(
        shape[:axis] + (2,) * bits + (shape[axis] // size,) + shape[axis + 1 :]
    )
    for bit in range(bits):
        parts = exchange_halves(parts, "sp", bit, axis + bits - 1 - bit)
    for bit in reversed(range(bits)):
        parts = gather_halves(parts, "sp", bit, axis + bits - 1 - bit)
    return parts.reshape(shape)


def settle_vectors(grads):
    size = lax.axis_size("fsdp")
    bits = log_two(size)
    parts = grads.reshape((2,) * bits + grads.shape[1:])
    for bit in range(bits):
        parts = exchange_halves(parts, "fsdp", bit, bits - 1 - bit)
    groups = lax.axis_size("sp")
    for bit in range(log_two(groups)):
        parts = parts + lax.ppermute(parts, "sp", [(i, i ^ (1 << bit)) for i in range(groups)])
    return parts


def settle(grads, axis):
    bits = log_two(lax.axis_size("fsdp"))
    half = grads.shape[1] // 2
    forward = [0] + list(range(1, bits))
    backward = [0] + list(range(bits - 1, 0, -1))
    low = grads.astype(jnp.bfloat16)
    first = reduce_owner(low[:, :half], forward)
    second = reduce_owner(low[:, half:], backward)
    return reduce_frames(jnp.concatenate([first, second], axis=1), axis)


def dot_of(left, right, left_dim, right_dim):
    return lax.dot_general(
        left, right, (((left_dim,), (right_dim,)), ((), ())), preferred_element_type=jnp.float32
    )


def attend_kernel(query_ref, key_ref, value_ref, mixed_ref, total_ref):
    head_size, length = key_ref.shape[1:]
    block = min(512, length)
    scale = head_size ** (-0.5)
    keys = key_ref[0]
    values = value_ref[0]
    for start in range(0, length, block):
        rows = slice(start, start + block)
        scores = dot_of(keys, query_ref[0, :, rows], 0, 0) * scale
        highest = jnp.max(scores, axis=0, keepdims=True)
        powered = jnp.exp(scores - highest)
        summed = jnp.sum(powered, axis=0, keepdims=True)
        weights_low = (powered * (1.0 / summed)).astype(jnp.bfloat16)
        mixed_ref[0, :, rows] = dot_of(values, weights_low, 1, 0).astype(jnp.bfloat16)
        total_ref[0, :, rows] = highest + jnp.log(summed)


def attend_back_kernel(
    query_ref, key_ref, value_ref, total_ref, grad_ref, dq_ref, dk_ref, dv_ref
):
    head_size, length = key_ref.shape[1:]
    block = min(512, length)
    scale = head_size ** (-0.5)
    keys = key_ref[0]
    values = value_ref[0]
    sum_keys = jnp.zeros((head_size, length), jnp.float32)
    sum_values = jnp.zeros((head_size, length), jnp.float32)
    for start in range(0, length, block):
        rows = slice(start, start + block)
        queries = query_ref[0, :, rows]
        grads = grad_ref[0, :, rows]
        weights = jnp.exp(dot_of(keys, queries, 0, 0) * scale - total_ref[0, :, rows])
        grad_weights = dot_of(values, grads, 0, 0)
        inner = jnp.sum(weights * grad_weights, axis=0, keepdims=True)
        grad_scores = (weights * (grad_weights - inner)).astype(jnp.bfloat16)
        dq_ref[0, :, rows] = (dot_of(keys, grad_scores, 1, 0) * scale).astype(jnp.bfloat16)
        sum_keys = sum_keys + dot_of(queries, grad_scores, 1, 1)
        sum_values = sum_values + dot_of(grads, weights.astype(jnp.bfloat16), 1, 1)
    dk_ref[0] = (sum_keys * scale).astype(jnp.bfloat16)
    dv_ref[0] = sum_values.astype(jnp.bfloat16)


def call_heads(kernel, operands, results):
    def spec(array):
        return pl.BlockSpec((1,) + array.shape[1:], lambda i: (i, 0, 0))

    return pl.pallas_call(
        kernel,
        grid=(operands[0].shape[0],),
        in_specs=[spec(array) for array in operands],
        out_specs=[spec(array) for array in results],
        out_shape=results,
        compiler_params=pltpu.CompilerParams(vmem_limit_bytes=40 * 1024 * 1024),
    )(*operands)


def attend(query_rows, key_rows, value_rows):
    count, _, length = query_rows.shape
    return call_heads(
        attend_kernel,
        (query_rows, key_rows, value_rows),
        (
            jax.ShapeDtypeStruct(query_rows.shape, jnp.bfloat16),
            jax.ShapeDtypeStruct((count, 1, length), jnp.float32),
        ),
    )


def attend_back(query_rows, key_rows, value_rows, log_total, grad_mixed):
    shape = jax.ShapeDtypeStruct(query_rows.shape, jnp.bfloat16)
    return call_heads(
        attend_back_kernel,
        (query_rows, key_rows, value_rows, log_total, grad_mixed),
        (shape, shape, shape),
    )


def local(
    inputs,
    w_qkv,
    w_out,
    w_up,
    w_down,
    norm_gain,
    norm_shift,
    qv_bias,
    branch_bias,
    up_bias,
    cotangent,
):
    clips, frames, width = inputs.shape
    groups = lax.axis_size("sp")
    length = frames * groups
    hidden = w_up.shape[2]
    local_heads = width // groups // HD
    rows_all = clips * frames
    stream = inputs.astype(jnp.float32).reshape(rows_all, width)
    kept = []
    shard = w_out.shape[1]
    vectors = jnp.concatenate(
        [
            part
            for l in range(LAYERS)
            for part in (
                norm_gain[l].T,
                norm_shift[l].T,
                qv_bias[l].T,
                branch_bias[l].T,
                up_bias[l].reshape(shard, -1),
            )
        ],
        axis=1,
    )
    count = vectors.shape[1] // LAYERS
    spare = 128 - vectors.shape[1]
    first = jnp.concatenate(
        [w_qkv[0].reshape(shard, -1), jnp.pad(vectors, ((0, 0), (0, spare)))], axis=1
    )
    first = gather_rows(first)
    vectors = first[:, 3 * width :]
    for layer_index in range(LAYERS):
        if layer_index == 0:
            weight_qkv = first[:, : 3 * width]
        else:
            weight_qkv = gather_rows(w_qkv[layer_index].reshape(shard, -1))
        both = gather_rows(jnp.concatenate([w_out[layer_index], w_up[layer_index]], axis=1))
        weight_out = both[:, :width]
        weight_up = both[:, width:]
        weight_down = gather_rows(w_down[layer_index])
        vector_full = vectors[:, layer_index * count : (layer_index + 1) * count].astype(
            jnp.float32
        )
        gains = vector_full[:, 0:2]
        shifts = vector_full[:, 2:4]
        attn_bias = vector_full[:, 4:6]
        branch = vector_full[:, 6:8]
        up_shift = vector_full[:, 8:].reshape(hidden)
        normed = norm_rows(stream, gains[:, 0], shifts[:, 0]).astype(jnp.bfloat16)
        bias_qkv = jnp.concatenate(
            [attn_bias[:, 0], jnp.zeros((width,), jnp.float32), attn_bias[:, 1]]
        )
        projected = (product(normed, weight_qkv) + bias_qkv).astype(jnp.bfloat16)
        heads = lax.all_to_all(
            jnp.transpose(projected.reshape(clips, frames, 3, width), (0, 2, 3, 1)),
            "sp",
            split_axis=2,
            concat_axis=3,
            tiled=True,
        )
        query_rows = heads[:, 0].reshape(clips * local_heads, HD, length)
        key_rows = heads[:, 1].reshape(clips * local_heads, HD, length)
        value_rows = heads[:, 2].reshape(clips * local_heads, HD, length)
        mixed, log_total = attend(query_rows, key_rows, value_rows)
        returned = lax.all_to_all(
            mixed.reshape(clips, width // groups, length),
            "sp",
            split_axis=2,
            concat_axis=1,
            tiled=True,
        )
        mixed_rows = jnp.swapaxes(returned, 1, 2).reshape(rows_all, width)
        middle = stream + product(mixed_rows, weight_out) + branch[:, 0]
        normed_two = norm_rows(middle, gains[:, 1], shifts[:, 1]).astype(jnp.bfloat16)
        pre_act = product(normed_two, weight_up) + up_shift
        activated = gelu_exact(pre_act).astype(jnp.bfloat16)
        kept.append(
            (
                stream,
                weight_qkv,
                weight_out,
                weight_up,
                weight_down,
                gains,
                shifts,
                normed,
                query_rows,
                key_rows,
                value_rows,
                log_total,
                mixed_rows,
                middle,
                normed_two,
                pre_act,
                activated,
            )
        )
        stream = middle + product(activated, weight_down) + branch[:, 1]
    output = stream.astype(jnp.bfloat16).reshape(clips, frames, width)
    grad_stream = cotangent.astype(jnp.float32).reshape(rows_all, width)
    layer_grads = []
    vector_sums = []
    for layer_index in reversed(range(LAYERS)):
        (
            layer_input,
            weight_qkv,
            weight_out,
            weight_up,
            weight_down,
            gains,
            shifts,
            normed,
            query_rows,
            key_rows,
            value_rows,
            log_total,
            mixed_rows,
            middle,
            normed_two,
            pre_act,
            activated,
        ) = kept[layer_index]
        grad_branch = grad_stream.astype(jnp.bfloat16)
        grad_down = settle(outer_sum(activated, grad_branch), 0)
        grad_down_bias = column_sums(grad_branch)
        grad_act = product_back(grad_branch, weight_down)
        grad_pre = jax.vjp(gelu_exact, pre_act)[1](grad_act)[0].astype(jnp.bfloat16)
        grad_up = settle(outer_sum(normed_two, grad_pre), 1)
        grad_up_bias = column_sums(grad_pre)
        grad_norm_two = product_back(grad_pre, weight_up)
        norm_pull = jax.vjp(norm_rows, middle, gains[:, 1], shifts[:, 1])[1]
        grad_middle, grad_gain_two, grad_shift_two = norm_pull(grad_norm_two)
        grad_middle = grad_middle + grad_stream
        grad_branch_one = grad_middle.astype(jnp.bfloat16)
        grad_out = outer_sum(mixed_rows, grad_branch_one)
        grad_out_bias = column_sums(grad_branch_one)
        grad_mixed = product_back(grad_branch_one, weight_out).astype(jnp.bfloat16)
        grad_heads = lax.all_to_all(
            jnp.swapaxes(grad_mixed.reshape(clips, frames, width), 1, 2),
            "sp",
            split_axis=1,
            concat_axis=2,
            tiled=True,
        )
        grad_heads = grad_heads.reshape(clips * local_heads, HD, length)
        grad_parts = attend_back(query_rows, key_rows, value_rows, log_total, grad_heads)
        stacked = jnp.stack(
            [part.reshape(clips, width // groups, length) for part in grad_parts], axis=1
        )
        grad_proj = lax.all_to_all(stacked, "sp", split_axis=3, concat_axis=2, tiled=True)
        grad_proj = jnp.transpose(grad_proj, (0, 3, 1, 2)).reshape(rows_all, 3 * width)
        grad_qkv = outer_sum(normed, grad_proj)
        proj_sums = column_sums(grad_proj)
        grad_norm_one = product_back(grad_proj, weight_qkv)
        norm_pull = jax.vjp(norm_rows, layer_input, gains[:, 0], shifts[:, 0])[1]
        grad_input, grad_gain_one, grad_shift_one = norm_pull(grad_norm_one)
        grad_stream = grad_middle + grad_input
        grad_attn = settle(jnp.concatenate([grad_qkv, grad_out], axis=1), 1)
        vector_grads = jnp.concatenate(
            [
                grad_gain_one,
                grad_gain_two,
                grad_shift_one,
                grad_shift_two,
                proj_sums[:width],
                proj_sums[2 * width :],
                grad_out_bias,
                grad_down_bias,
            ]
        ).reshape(8, -1, shard)
        vector_grads = jnp.concatenate(
            [jnp.swapaxes(vector_grads, 0, 1), grad_up_bias.reshape(width // shard, -1, shard)],
            axis=1,
        )
        layer_grads.append((grad_attn, grad_up, grad_down))
        vector_sums.append(vector_grads)
    layer_grads = layer_grads[::-1]
    grad_inputs = grad_stream.astype(jnp.bfloat16).reshape(clips, frames, width)
    qkv_list, out_list, up_list, down_list = ([], [], [], [])
    gain_list, shift_list, bias_list, branch_list, upbias_list = ([], [], [], [], [])
    vector_sums = settle_vectors(jnp.concatenate(vector_sums[::-1], axis=1))
    for layer_index, (attn_part, up_part, down_part) in enumerate(layer_grads):
        vector_part = vector_sums[layer_index * count : (layer_index + 1) * count]
        attn_part = attn_part.astype(jnp.float32)
        qkv_list.append(attn_part[:, : 3 * width].reshape(shard, 3, width))
        out_list.append(attn_part[:, 3 * width :])
        up_list.append(up_part.astype(jnp.float32))
        down_list.append(down_part.astype(jnp.float32))
        gain_list.append(vector_part[0:2])
        shift_list.append(vector_part[2:4])
        bias_list.append(vector_part[4:6])
        branch_list.append(vector_part[6:8])
        upbias_list.append(vector_part[8:].reshape(-1))
    return (
        output,
        grad_inputs,
        jnp.stack(qkv_list),
        jnp.stack(out_list),
        jnp.stack(up_list),
        jnp.stack(down_list),
        jnp.stack(gain_list),
        jnp.stack(shift_list),
        jnp.stack(bias_list),
        jnp.stack(branch_list),
        jnp.stack(upbias_list),
    )


def solution(mesh):
    placed = (
        P("fsdp", "sp", None),
        P(None, "fsdp", None, None),
        P(None, "fsdp", None),
        P(None, "fsdp", None),
        P(None, "fsdp", None),
        P(None, None, "fsdp"),
        P(None, None, "fsdp"),
        P(None, None, "fsdp"),
        P(None, None, "fsdp"),
        P(None, "fsdp"),
        P("fsdp", "sp", None),
    )
    return jax.shard_map(
        local,
        mesh=mesh,
        in_specs=placed,
        out_specs=(
            P("fsdp", "sp", None),
            P("fsdp", "sp", None),
            P(None, "fsdp", None, None),
            P(None, "fsdp", None),
            P(None, "fsdp", None),
            P(None, "fsdp", None),
            P(None, None, "fsdp"),
            P(None, None, "fsdp"),
            P(None, None, "fsdp"),
            P(None, None, "fsdp"),
            P(None, "fsdp"),
        ),
        check_vma=False,
    )
```
